32 devices in a mesh: groups: 2 (over y), pencil: 4 (over x, core), point: 4 (over z).
Axes of the slice: x: 2, y: 2, z: 4, core: 2. Of those that a mesh axis runs over, the one named last changes fastest.
Arguments:
- point_features: bfloat16 [64, 262144], P(None, ('groups', 'pencil', 'point')), parts along dimension 1, may hold values from -6 to 6
- point_position: float32 [3, 262144], P(None, ('groups', 'pencil', 'point')), parts along dimension 1, may hold values from 0 to 1
- block_counts: int32 [32, 64], P(('groups', 'pencil', 'point')), parts along dimension 0, may hold values from 1 to 3, 128 in all within a row
- pair_tile: int32 [4096], P(('groups', 'pencil', 'point')), parts along dimension 0, may hold values from 0 to 4095, as said below
- pair_offset: float32 [3, 4096], P(None, ('groups', 'pencil', 'point')), parts along dimension 1, may hold values from -1 to 1
- skip_weight: bfloat16 [64, 64], replicated, may hold values from -0.75 to 0.75
- spectral_weight: bfloat16 [64, 32, 64, 128], P('pencil'), may hold values from -2.09375 to 2.09375
Outputs:
- encoded: bfloat16 [512, 256, 2048], P(('groups', 'pencil'), None, 'point'), parts along dimension 0
The draws below stay inside these ranges and needn't reach their ends.
There are 2 independent parts, one for each index of `groups`. The reference program is written for one: setup_inputs(seed, part) draws one part's arguments, and reference() takes and returns one part's arrays. A program takes and returns all parts, laid end to end along the dimension named above; an argument that names none is the same for every part. Nothing has to cross between parts.
Inputs may be any that keep to these rules, and one draw needn't show every extreme that they name: pair_tile // 1024 is the point index of the tile's owner in the same pencil row. The pairs of one device name tiles of one owner at most 32 times; in every pencil row some owner is named exactly 32 times by every device of that row. `block_counts`: the counts of one device sum to 128; a device's pairs are listed block by block, block 0 first.
All inputs are finite; a program needn't handle non-finite values.
Results may differ from the reference program's by a relative error of at most 0.005.
Values may be sent and summed in bfloat16 or wider, within the bound.
A program may use at most 256 MiB of HBM per device.

```python
import math
import jax
import jax.numpy as jnp
import numpy as np
from jax import lax

C = 64
NX = 256
NY = 256
MODES = 32
BLOCK = 128
TILE_CELLS = 128
KMAX = 3
ZL = 8
BLK_DEV = 64
KMODES = 64
TX = 64
TY = 2
TILES_DEV = 1024
PAIRS_DEV = 128
CAP = 32
PTS_DEV = 8192
ZS = 32
SEGS = 16
POINTS = 131072
PAIRS = 2048
N_PENCIL = 4
N_POINT = 4


def draw_pair_tile(key, part):
    key = jax.random.fold_in(key, 11)
    rows = N_PENCIL * N_POINT
    group_keys = jax.random.split(jax.random.fold_in(key, 1), N_PENCIL)

    def pick_heavy(group_key):
        return jax.random.randint(group_key, (), 0, N_POINT)
    heavy_owner = jax.vmap(pick_heavy)(group_keys)
    heavy_rows = jnp.repeat(heavy_owner, N_POINT)
    row_keys = jax.random.split(jax.random.fold_in(key, 2), rows)

    def one_row(row_key, heavy):
        first, second, third = jax.random.split(row_key, 3)
        spare = (N_POINT - 1) * CAP
        picked = jax.random.permutation(first, spare)[:PAIRS_DEV - CAP]
        others = (picked // CAP).astype(jnp.int32)
        others = others + (others >= heavy).astype(jnp.int32)
        owner_list = jnp.concatenate([jnp.full((CAP,), heavy, jnp.int32), others])
        owner_list = jax.random.permutation(second, owner_list)
        within = jax.random.randint(third, (PAIRS_DEV,), 0, TILES_DEV)
        return (owner_list * TILES_DEV + within).astype(jnp.int32)
    return jax.vmap(one_row)(row_keys, heavy_rows).reshape(-1)


def level_of(own_key, dims, cuts, least, largest):
    def one(dim, blocks):
        draws = jax.random.uniform(jax.random.fold_in(jax.random.fold_in(own_key, 6), dim), (blocks,), jnp.float32, least / len(cuts), largest / len(cuts))
        return jnp.repeat(jnp.exp(draws), dims[dim] // blocks).reshape((-1,) + (1,) * (len(dims) - dim - 1))

    gain = one(*cuts[0])
    for cut in cuts[1:]:
        gain = gain * one(*cut)
    return gain


def profile(number_of, total, limit, lean):
    weights = [(1 << 20) // math.isqrt(grade ** lean) + 1 for grade in range(2, number_of + 1)]
    rest, given = total - limit - (number_of - 1), [1] * (number_of - 1)
    while rest > 0:
        candidates = [i for i in range(number_of - 1) if given[i] < limit]
        pool, left = sum([weights[i] for i in candidates]), rest
        for i in candidates:
            addition = min(limit - given[i], max(1, left * weights[i] // pool), rest)
            given[i] = given[i] + addition
            rest = rest - addition
    return np.array([limit] + given)


def uneven_parts(rng, amount, total, reach, skew):
    if amount == 2:
        one = jax.random.randint(rng, (), max(1, total - reach), min(reach, total - 1) + 1)
        return jnp.stack([one, total - one])
    tallies = jnp.asarray(profile(amount, total, reach, skew), jnp.int32)
    pairs = (amount - 1) // 2
    source_of, sink = tallies[1:1 + 2 * pairs:2], tallies[2:2 + 2 * pairs:2]
    margin = jnp.minimum(source_of - 1, reach - sink)
    shifted = jax.random.randint(jax.random.fold_in(rng, 1), (pairs,), 0, 1 << 20) % (margin + 1)
    tallies = tallies.at[1:1 + 2 * pairs:2].set(source_of - shifted).at[2:2 + 2 * pairs:2].set(sink + shifted)
    return tallies[jax.random.permutation(jax.random.fold_in(rng, 2), amount)]


def noise(key, dims, spread, limit, shards=(), held_as=jnp.bfloat16):
    entries = spread * jax.random.normal(key, dims, jnp.float32)
    if shards:
        entries = entries * level_of(key, dims, shards, -0.22, 0.18)
    return jnp.clip(entries, -limit, limit).astype(held_as)


def setup_inputs(seed: int = 0, part: int = 0) -> dict:
    seeds = jax.random.split(jax.random.key(seed), 8)
    own_keys = jax.random.split(jax.random.fold_in(seeds[7], part), 8)
    return {
        "point_features": noise(own_keys[0], (C, POINTS), 1.0, 6.0, ((1, 16),)),
        "point_position": jnp.clip(1.0 * jax.random.uniform(own_keys[1], (3, POINTS), jnp.float32) ** level_of(own_keys[1], (3, POINTS), ((1, 16),), -0.2, 0.2), 0.0, 1.0),
        "block_counts": jax.vmap(lambda own: uneven_parts(own, BLK_DEV, PAIRS_DEV, KMAX, 0))(jax.random.split(own_keys[2], SEGS)).reshape((SEGS, BLK_DEV)).astype(jnp.int32),
        "pair_tile": draw_pair_tile(jax.random.fold_in(jax.random.fold_in(seeds[7], part), 71), part),
        "pair_offset": jnp.clip(jax.random.uniform(own_keys[4], (3, PAIRS), jnp.float32, -1.0, 1.0) * level_of(own_keys[4], (3, PAIRS), ((1, 16),), -0.4, 0.0), -1.0, 1.0),
        "skip_weight": noise(seeds[5], (C, C), C ** -0.5, 0.75),
        "spectral_weight": noise(seeds[6], (KMODES, MODES, C, 2 * C), 0.35, 2.09375, ((0, 4),)),
    }


def kernel_weights(spot_rows, offsets, tile_width, tile_height):
    cell_index = jnp.arange(tile_width * tile_height, dtype=jnp.int32)
    cell_x = (cell_index // tile_height).astype(jnp.float32) + 0.5
    cell_y = (cell_index % tile_height).astype(jnp.float32) + 0.5
    point_x = spot_rows[0] * float(tile_width) + offsets[0][:, None]
    point_y = spot_rows[1] * float(tile_height) + offsets[1][:, None]
    point_z = spot_rows[2] - 0.5 + offsets[2][:, None]
    gap_x = point_x[:, None, :] - cell_x[None, :, None]
    gap_y = point_y[:, None, :] - cell_y[None, :, None]
    distance = gap_x * gap_x + gap_y * gap_y + (point_z * point_z)[:, None, :]
    return jnp.exp(-distance).astype(jnp.bfloat16)


def device_terms(features, position, block_sizes, offsets):
    pairs_dev = offsets.shape[1]
    block_ends = jnp.cumsum(block_sizes).astype(jnp.int32)
    pair_order = jnp.arange(pairs_dev, dtype=jnp.int32)
    block_of = jnp.sum((block_ends[None, :] <= pair_order[:, None]).astype(jnp.int32), axis=1)
    chosen_rows = jnp.take(features.reshape(C, BLK_DEV, BLOCK), block_of, axis=1)
    spot_rows = jnp.take(position.reshape(3, BLK_DEV, BLOCK), block_of, axis=1)
    weights = kernel_weights(spot_rows, offsets, TX, TY)
    terms = jnp.einsum('cpj,pkj->pck', chosen_rows.astype(jnp.float32), weights.astype(jnp.float32))
    return terms.astype(jnp.bfloat16)


def reference(point_features, point_position, block_counts, pair_tile, pair_offset, skip_weight, spectral_weight):
    features = point_features.reshape(C, N_PENCIL, N_POINT, PTS_DEV).transpose(1, 2, 0, 3)
    position = point_position.reshape(3, N_PENCIL, N_POINT, PTS_DEV).transpose(1, 2, 0, 3)
    counts = block_counts.reshape(N_PENCIL, N_POINT, BLK_DEV)
    tiles = pair_tile.reshape(N_PENCIL, N_POINT, PAIRS_DEV)
    offsets = pair_offset.reshape(3, N_PENCIL, N_POINT, PAIRS_DEV).transpose(1, 2, 0, 3)

    def pencil_row(inputs):
        row_features, row_position, row_counts, row_tiles, row_offsets = inputs
        terms = jax.vmap(device_terms)(row_features, row_position, row_counts, row_offsets)
        flat_terms = terms.reshape(N_POINT * PAIRS_DEV, C * TILE_CELLS).astype(jnp.float32)
        sums = jax.ops.segment_sum(flat_terms, row_tiles.reshape(-1), num_segments=N_POINT * TILES_DEV)
        grid = sums.astype(jnp.bfloat16).reshape(N_POINT, ZL, NY // TY, C, TX, TY)
        return grid.transpose(4, 2, 5, 0, 1, 3).reshape(TX, NY, ZS * C)

    latent = lax.map(pencil_row, (features, position, counts, tiles, offsets)).reshape(NX, NY, ZS * C)
    weight = spectral_weight.astype(jnp.float32)
    complex_weight = weight[..., :C] + 1j * weight[..., C:]

    def layer_block(owner):
        block = lax.dynamic_slice_in_dim(latent, owner * (ZL * C), ZL * C, axis=2)
        field = block.astype(jnp.float32)
        spec = jnp.fft.fft(jnp.fft.rfft(field, axis=1)[:, :MODES], axis=0)
        kept = jnp.concatenate([spec[:MODES], spec[NX - MODES:]], axis=0).reshape(KMODES, MODES, ZL, C)
        mixed = jnp.einsum('kmzi,kmio->kmzo', kept, complex_weight, precision=lax.Precision.HIGHEST)
        full = jnp.zeros((NX, NY // 2 + 1, ZL, C), dtype=mixed.dtype)
        full = full.at[:MODES, :MODES].set(mixed[:MODES])
        full = full.at[NX - MODES:, :MODES].set(mixed[MODES:])
        wave = jnp.fft.irfft2(full, s=(NX, NY), axes=(0, 1))
        skip = jnp.einsum('xyzi,io->xyzo', field.reshape(NX, NY, ZL, C), skip_weight.astype(jnp.float32))
        return jax.nn.gelu(wave + skip, approximate=False).astype(jnp.bfloat16).reshape(NX, NY, ZL * C)

    blocks = lax.map(layer_block, jnp.arange(N_POINT, dtype=jnp.int32))
    return blocks.transpose(1, 2, 0, 3).reshape(NX, NY, ZS * C)
```

```python
import functools
import math

import jax
import jax.numpy as jnp
from jax import lax
from jax.experimental import pallas as pl
from jax.experimental.pallas import tpu as pltpu
from jax.sharding import PartitionSpec as P

NX = 256
NY = 256
MODES = 32
BLOCK = 128
TILE_CELLS = 128
ZL = 8
KMODES = 64
CAP = 32
HALF_Z = ZL // 2
LANES = 128
VMEM_LIMIT = 56 * 1024 * 1024


def dot(left, right):
    return jnp.dot(left, right, preferred_element_type=jnp.float32)


def terms_kernel(tiles_dev, counts, tiles, offsets, features, position, out, used):
    slots, width, lanes = out.shape
    channels = features.shape[0]
    height = lanes // channels
    owners = slots // CAP
    pairs = tiles.shape[0]
    for owner in range(owners):
        used[owner] = 0
    out[...] = jnp.zeros_like(out)
    cell_x = lax.broadcasted_iota(jnp.int32, (width, BLOCK), 0).astype(jnp.float32) + 0.5

    def one(pair, carry):
        block, end = carry
        moved = (pair >= end).astype(jnp.int32)
        block = block + moved
        end = end + moved * counts[0, block]
        at = pl.ds(pl.multiple_of(block * BLOCK, BLOCK), BLOCK)
        spot = position[:, at]
        gap_x = spot[0:1] * float(width) + offsets[0, pair] - cell_x
        along_x = jnp.exp(-(gap_x * gap_x))
        point_y = spot[1:2] * float(height) + offsets[1, pair]
        point_z = spot[2:3] - 0.5 + offsets[2, pair]
        square_z = point_z * point_z
        rows = []
        for row in range(height):
            gap_y = point_y - (row + 0.5)
            rows.append((along_x * jnp.exp(-(gap_y * gap_y + square_z))).astype(jnp.bfloat16))
        cells = jnp.concatenate(rows, axis=0)
        term = lax.dot_general(
            cells, features[:, at], (((1,), (1,)), ((), ())), preferred_element_type=jnp.float32
        )
        term = jnp.concatenate(
            [term[row * width : (row + 1) * width] for row in range(height)], axis=1
        )
        owner = tiles[pair] // tiles_dev
        slot = used[owner]
        used[owner] = slot + 1
        out[owner * CAP + slot] = term.astype(jnp.bfloat16)
        return block, end

    lax.fori_loop(0, pairs, one, (jnp.int32(0), counts[0, 0]), unroll=4)


def make_terms(features, position, counts, tiles, offsets, owners, width, height, tiles_dev):
    channels = features.shape[0]
    smem = pl.BlockSpec(memory_space=pltpu.SMEM)
    vmem = pl.BlockSpec(memory_space=pltpu.VMEM)
    return pl.pallas_call(
        functools.partial(terms_kernel, tiles_dev),
        out_shape=jax.ShapeDtypeStruct((owners * CAP, width, height * channels), jnp.bfloat16),
        in_specs=[smem, smem, smem, vmem, vmem],
        out_specs=vmem,
        scratch_shapes=[pltpu.SMEM((owners,), jnp.int32)],
        compiler_params=pltpu.CompilerParams(vmem_limit_bytes=VMEM_LIMIT),
    )(counts, tiles, offsets, features, position)


def forward_kernel(height, arrived, x_wave, y_wave, out, held):
    slots, width, lanes = arrived.shape
    parts, _ = x_wave.shape[1:]
    steps = parts // 2
    rows = out.shape[1]
    channels = lanes // height
    groups = lanes // LANES

    def one(slot, carry):
        wave = dot(x_wave[0], arrived[slot])
        for group in range(groups):
            held[group, pl.ds(slot, parts, stride=slots), :] = wave[
                :, group * LANES : (group + 1) * LANES
            ]
        return carry

    lax.fori_loop(0, slots, one, 0, unroll=4)

    def mode(index, carry):
        both = [
            jnp.concatenate(
                [
                    held[
                        group,
                        pl.ds(pl.multiple_of((index + part * steps) * slots, slots), slots),
                        :,
                    ]
                    for part in range(2)
                ],
                axis=0,
            ).astype(jnp.bfloat16)
            for group in range(groups)
        ]
        real_sum = None
        for row in range(height):
            group, first = divmod(row * channels, LANES)
            piece = dot(y_wave[row], both[group][:, first : first + channels])
            real_sum = piece if real_sum is None else real_sum + piece
        out[index] = jnp.concatenate([real_sum[:rows], real_sum[rows:]], axis=1).astype(
            jnp.bfloat16
        )
        return carry

    lax.fori_loop(0, steps, mode, 0, unroll=2)


def forward(arrived, x_wave, y_wave, height, chunk):
    slots, width, lanes = arrived.shape
    channels = lanes // height
    rows = y_wave.shape[1] // 2
    steps = KMODES // chunk
    whole = lambda shape: pl.BlockSpec(shape, lambda step: (0,) * len(shape))
    return pl.pallas_call(
        functools.partial(forward_kernel, height),
        grid=(steps,),
        out_shape=jax.ShapeDtypeStruct((KMODES, rows, 2 * channels), jnp.bfloat16),
        in_specs=[
            whole(arrived.shape),
            pl.BlockSpec((1, 2 * chunk, width), lambda step: (step, 0, 0)),
            whole(y_wave.shape),
        ],
        out_specs=pl.BlockSpec((chunk, rows, 2 * channels), lambda step: (step, 0, 0)),
        scratch_shapes=[pltpu.VMEM((lanes // LANES, 2 * chunk * slots, LANES), jnp.float32)],
        compiler_params=pltpu.CompilerParams(vmem_limit_bytes=VMEM_LIMIT),
    )(arrived, x_wave, y_wave)


def mix_kernel(spectra, weight, out, held):
    sources, _, rows, lanes = spectra.shape
    count = pl.num_programs(0)
    step = pl.program_id(0)
    stride = held.shape[0] // rows
    channels = lanes // 2
    row = lax.broadcasted_iota(jnp.int32, (ZL, lanes), 0)
    lane = lax.broadcasted_iota(jnp.int32, (ZL, lanes), 1)
    keep = (row < HALF_Z) == (lane < channels)
    for mode in range(MODES):
        at = slice(mode * ZL, (mode + 1) * ZL)
        total = spectra[0, 0, at].astype(jnp.float32)
        for source in range(1, sources):
            total = total + spectra[source, 0, at].astype(jnp.float32)
        plain = weight[0, mode]
        turned = jnp.concatenate([-plain[:, channels:], plain[:, :channels]], axis=1)
        mixed = dot(total.astype(jnp.bfloat16), jnp.concatenate([plain, turned], axis=0))
        other = pltpu.roll(pltpu.roll(mixed, HALF_Z, 0), channels, 1)
        held[pl.ds(mode * ZL * stride + step, ZL, stride=stride), :] = jnp.where(
            keep, mixed, other
        )

    @pl.when(step == count - 1)
    def _():
        out[...] = held[...].reshape(out.shape).astype(jnp.bfloat16)


def mix(spectra, weight):
    sources, own, rows, lanes = spectra.shape
    return pl.pallas_call(
        mix_kernel,
        grid=(own,),
        out_shape=jax.ShapeDtypeStruct((rows, own, lanes), jnp.bfloat16),
        in_specs=[
            pl.BlockSpec((sources, 1, rows, lanes), lambda step: (0, step, 0, 0)),
            pl.BlockSpec((1,) + weight.shape[1:], lambda step: (step, 0, 0, 0)),
        ],
        out_specs=pl.BlockSpec((rows, own, lanes), lambda step: (0, 0, 0)),
        scratch_shapes=[pltpu.VMEM((rows * own, lanes), jnp.float32)],
        compiler_params=pltpu.CompilerParams(vmem_limit_bytes=VMEM_LIMIT),
    )(spectra, weight)


def backward_kernel(height, mixed, terms, x_back, y_back, layer_mask, skip, out, held):
    sources, rows, own, lanes = mixed.shape
    width = x_back.shape[0] // 2
    channels = lanes // 2
    per_step = out.shape[0]
    step = pl.program_id(0)

    @pl.when(step == 0)
    def _():
        def mode(index, carry):
            for layer in range(HALF_Z):
                modes = jnp.concatenate(
                    [
                        mixed[source, index * ZL + part * HALF_Z + layer]
                        for part in range(2)
                        for source in range(sources)
                    ],
                    axis=0,
                )
                held[layer, pl.ds(index, 2 * width, stride=MODES), :] = dot(x_back[...], modes)
            return carry

        lax.fori_loop(0, MODES, mode, 0, unroll=2)

    for inner in range(per_step):
        x = step * per_step + inner
        parts = [
            jnp.concatenate(
                [
                    held[
                        layer,
                        pl.ds(pl.multiple_of((part * width + x) * MODES, MODES), MODES),
                        :,
                    ]
                    for layer in range(HALF_Z)
                ],
                axis=1,
            ).astype(jnp.bfloat16)
            for part in range(2)
        ]
        skipped = dot(terms[inner], skip[...]).astype(jnp.bfloat16)
        for row in range(height):
            piece = skipped[:, row * channels : (row + 1) * channels]
            pair = jnp.concatenate([piece, piece], axis=1)
            parts.append(jnp.concatenate([pair] * HALF_Z, axis=1) * layer_mask[...])
        value = dot(y_back[...], jnp.concatenate(parts, axis=0))
        out[inner] = (0.5 * value * (1.0 + lax.erf(value * math.sqrt(0.5)))).astype(jnp.bfloat16)


def backward(mixed, terms, x_back, y_back, layer_mask, skip, height, per_step):
    width, slots, lanes = terms.shape
    whole = lambda shape: pl.BlockSpec(shape, lambda step: (0,) * len(shape))
    depth = layer_mask.shape[1]
    return pl.pallas_call(
        functools.partial(backward_kernel, height),
        grid=(width // per_step,),
        out_shape=jax.ShapeDtypeStruct((width, NY, depth), jnp.bfloat16),
        in_specs=[
            whole(mixed.shape),
            pl.BlockSpec((per_step, slots, lanes), lambda step: (step, 0, 0)),
            whole(x_back.shape),
            whole(y_back.shape),
            whole(layer_mask.shape),
            whole(skip.shape),
        ],
        out_specs=pl.BlockSpec((per_step, NY, depth), lambda step: (step, 0, 0)),
        scratch_shapes=[pltpu.VMEM((HALF_Z, 2 * width * MODES, mixed.shape[3]), jnp.float32)],
        compiler_params=pltpu.CompilerParams(vmem_limit_bytes=VMEM_LIMIT),
    )(mixed, terms, x_back, y_back, layer_mask, skip)


def angle(phase, length):
    return (phase % length).astype(jnp.float32) * (2.0 * math.pi / length)


def per_device(
    point_features,
    point_position,
    block_counts,
    pair_tile,
    pair_offset,
    skip_weight,
    spectral_weight,
):
    pencils = lax.axis_size("pencil")
    owners = lax.axis_size("point")
    pencil = lax.axis_index("pencil")
    me = lax.axis_index("point")
    channels = skip_weight.shape[0]
    width = NX // pencils
    height = TILE_CELLS // width
    row_blocks = NY // height
    tiles_dev = ZL * row_blocks
    slots = owners * CAP
    own = KMODES // pencils
    bf16 = jnp.bfloat16

    row_tiles = lax.all_gather(pair_tile, "point")
    terms = make_terms(
        point_features,
        point_position,
        block_counts,
        pair_tile,
        pair_offset,
        owners,
        width,
        height,
        tiles_dev,
    )
    arrived = lax.all_to_all(terms, "point", split_axis=0, concat_axis=0, tiled=True)

    mine = (row_tiles // tiles_dev == me).astype(jnp.int32)
    place = jnp.cumsum(mine, axis=1) - 1
    hit = (place[:, :, None] == jnp.arange(CAP, dtype=jnp.int32)) & (mine[:, :, None] == 1)
    labels = (
        jnp.sum(jnp.where(hit, (row_tiles % tiles_dev + 1)[:, :, None], 0), axis=1) - 1
    ).reshape(slots)
    layer_of = jnp.where(labels >= 0, labels // row_blocks, -1)
    block_of = labels % row_blocks

    modes = jnp.arange(MODES, dtype=jnp.int32)
    x_index = jnp.arange(KMODES, dtype=jnp.int32)
    x_freqs = jnp.where(x_index < MODES, x_index, NX - KMODES + x_index)
    x_cells = pencil * width + jnp.arange(width, dtype=jnp.int32)
    x_angle = angle(x_freqs[:, None] * x_cells[None, :], NX)
    x_cos, x_sin = jnp.cos(x_angle), jnp.sin(x_angle)
    chunk = KMODES if slots * height * channels * KMODES * 8 <= 16 * 1024 * 1024 else 8
    steps = KMODES // chunk
    x_wave = (
        jnp.stack([x_cos, -x_sin])
        .reshape(2, steps, chunk, width)
        .transpose(1, 0, 2, 3)
        .reshape(steps, 2 * chunk, width)
        .astype(bf16)
    )
    x_back = jnp.concatenate(
        [
            jnp.concatenate([x_cos.T, -x_sin.T], axis=1),
            jnp.concatenate([x_sin.T, x_cos.T], axis=1),
        ],
        axis=0,
    ).astype(bf16)

    pair_y = block_of[None, :] * height + jnp.arange(height, dtype=jnp.int32)[:, None]
    y_angle = angle(modes[None, :, None] * pair_y[:, None, :], NY)
    y_cos, y_sin = jnp.cos(y_angle).astype(bf16), jnp.sin(y_angle).astype(bf16)
    order = jnp.arange(ZL, dtype=jnp.int32)
    order = order % HALF_Z * 2 + order // HALF_Z
    layer_hit = layer_of[None, :] == order[:, None]
    turned = jnp.stack(
        [
            jnp.stack([y_cos, y_sin], axis=2),
            jnp.stack([-y_sin, y_cos], axis=2),
        ],
        axis=1,
    )
    y_wave = jnp.where(
        layer_hit[None, None, None, :, None, :], turned[:, :, :, None], jnp.zeros((), bf16)
    ).reshape(height, 2 * MODES * ZL, 2 * slots)

    rows_y = jnp.arange(NY, dtype=jnp.int32)
    back_angle = angle(rows_y[:, None] * modes[None, :], NY)
    scale = jnp.where(modes == 0, 1.0, 2.0).astype(jnp.float32)[None, :] / (NX * NY)
    y_back = jnp.concatenate(
        [
            (jnp.cos(back_angle) * scale).astype(bf16),
            (-jnp.sin(back_angle) * scale).astype(bf16),
            (rows_y[:, None] == pair_y.reshape(-1)[None, :]).astype(bf16),
        ],
        axis=1,
    )
    lane_layer = jnp.arange(ZL * channels, dtype=jnp.int32) // channels
    layer_mask = (layer_of[:, None] == lane_layer[None, :]).astype(bf16)
    skip = jnp.kron(jnp.eye(height, dtype=bf16), skip_weight)

    partial = forward(arrived, x_wave, y_wave, height, chunk)
    spectra = lax.all_to_all(partial, "pencil", split_axis=0, concat_axis=0, tiled=True)
    mixed = mix(spectra.reshape(pencils, own, MODES * ZL, 2 * channels), spectral_weight)
    gathered = lax.all_gather(mixed, "pencil")
    by_row = arrived.transpose(1, 0, 2)
    return backward(
        gathered, by_row, x_back, y_back, layer_mask, skip, height, 4 if width % 4 == 0 else 1
    )


def solution(mesh):
    placed = (
        P(None, ("groups", "pencil", "point")),
        P(None, ("groups", "pencil", "point")),
        P(("groups", "pencil", "point"), None),
        P(("groups", "pencil", "point")),
        P(None, ("groups", "pencil", "point")),
        P(),
        P("pencil", None, None, None),
    )
    return jax.shard_map(
        per_device,
        mesh=mesh,
        in_specs=placed,
        out_specs=P(("groups", "pencil"), None, "point"),
        check_vma=False,
    )
```

```python
import functools
import math

import jax
import jax.numpy as jnp
from jax import lax
from jax.experimental import pallas as pl
from jax.experimental.pallas import tpu as pltpu
from jax.sharding import PartitionSpec as P

NX = 256
NY = 256
MODES = 32
BLOCK = 128
TILE_CELLS = 128
ZL = 8
KMODES = 64
CAP = 32
HALF_Z = ZL // 2
LANES = 128
VMEM_LIMIT = 56 * 1024 * 1024


def dot(left, right):
    return jnp.dot(left, right, preferred_element_type=jnp.float32)


def terms_kernel(tiles_dev, counts, tiles, offsets, features, position, out, used):
    slots, width, lanes = out.shape
    channels = features.shape[0]
    height = lanes // channels
    owners = slots // CAP
    pairs = tiles.shape[0]
    for owner in range(owners):
        used[owner] = 0
    out[...] = jnp.zeros_like(out)
    cell_x = lax.broadcasted_iota(jnp.int32, (width, BLOCK), 0).astype(jnp.float32) + 0.5

    def one(pair, carry):
        block, end = carry
        moved = (pair >= end).astype(jnp.int32)
        block = block + moved
        end = end + moved * counts[0, block]
        at = pl.ds(pl.multiple_of(block * BLOCK, BLOCK), BLOCK)
        spot = position[:, at]
        gap_x = spot[0:1] * float(width) + offsets[0, pair] - cell_x
        along_x = jnp.exp(-(gap_x * gap_x))
        point_y = spot[1:2] * float(height) + offsets[1, pair]
        point_z = spot[2:3] - 0.5 + offsets[2, pair]
        square_z = point_z * point_z
        rows = []
        for row in range(height):
            gap_y = point_y - (row + 0.5)
            rows.append((along_x * jnp.exp(-(gap_y * gap_y + square_z))).astype(jnp.bfloat16))
        cells = jnp.concatenate(rows, axis=0)
        term = lax.dot_general(
            cells, features[:, at], (((1,), (1,)), ((), ())), preferred_element_type=jnp.float32
        )
        term = jnp.concatenate(
            [term[row * width : (row + 1) * width] for row in range(height)], axis=1
        )
        owner = tiles[pair] // tiles_dev
        slot = used[owner]
        used[owner] = slot + 1
        out[owner * CAP + slot] = term.astype(jnp.bfloat16)
        return block, end

    lax.fori_loop(0, pairs, one, (jnp.int32(0), counts[0, 0]), unroll=4)


def make_terms(features, position, counts, tiles, offsets, owners, width, height, tiles_dev):
    channels = features.shape[0]
    smem = pl.BlockSpec(memory_space=pltpu.SMEM)
    vmem = pl.BlockSpec(memory_space=pltpu.VMEM)
    return pl.pallas_call(
        functools.partial(terms_kernel, tiles_dev),
        out_shape=jax.ShapeDtypeStruct((owners * CAP, width, height * channels), jnp.bfloat16),
        in_specs=[smem, smem, smem, vmem, vmem],
        out_specs=vmem,
        scratch_shapes=[pltpu.SMEM((owners,), jnp.int32)],
        compiler_params=pltpu.CompilerParams(vmem_limit_bytes=VMEM_LIMIT),
    )(counts, tiles, offsets, features, position)


def forward_kernel(height, arrived, x_wave, y_wave, out, held):
    slots, width, lanes = arrived.shape
    parts = x_wave.shape[1]
    steps = parts // 2
    rows = out.shape[1]
    groups = lanes // LANES
    channels = lanes // height
    per_group = LANES // channels
    stride = held.shape[1] // parts
    first_half = lax.broadcasted_iota(jnp.int32, (1, LANES), 1) < channels

    def one(slot, carry):
        cells = arrived[slot]
        wave = dot(x_wave[0], jnp.concatenate([cells, cells], axis=0))
        for group in range(groups):
            held[group, pl.ds(slot, parts, stride=stride), :] = wave[
                :, group * LANES : (group + 1) * LANES
            ]
        return carry

    lax.fori_loop(0, slots, one, 0, unroll=8)

    def both(index, group):
        return jnp.concatenate(
            [
                held[
                    group,
                    pl.ds(pl.multiple_of((index + part * steps) * stride, 8), slots),
                    :,
                ]
                for part in range(2)
            ],
            axis=0,
        )

    def modes(index, carry):
        base = index * 4
        columns = []
        for pair in range(2):
            pieces = []
            for group in range(groups):
                left, right = both(base + 2 * pair, group), both(base + 2 * pair + 1, group)
                left_turned = pltpu.roll(left, channels, 1)
                right_turned = pltpu.roll(right, channels, 1)
                pieces.append(jnp.where(first_half, left, right_turned).astype(jnp.bfloat16))
                pieces.append(jnp.where(first_half, left_turned, right).astype(jnp.bfloat16))
            columns.append(jnp.concatenate(pieces, axis=0))
        total = dot(y_wave[...], jnp.concatenate(columns, axis=1))
        for pair in range(2):
            real = total[:rows, pair * LANES : (pair + 1) * LANES]
            imag = total[rows:, pair * LANES : (pair + 1) * LANES]
            out[base + 2 * pair] = jnp.where(
                first_half, real, pltpu.roll(imag, channels, 1)
            ).astype(jnp.bfloat16)
            out[base + 2 * pair + 1] = jnp.where(
                first_half, pltpu.roll(real, channels, 1), imag
            ).astype(jnp.bfloat16)
        return carry

    lax.fori_loop(0, steps // 4, modes, 0)


def forward(arrived, x_wave, y_wave, height):
    slots, width, lanes = arrived.shape
    channels = lanes // height
    rows = y_wave.shape[0] // 2
    steps, double, depth = x_wave.shape
    chunk = double // 2
    whole = lambda shape: pl.BlockSpec(shape, lambda step: (0,) * len(shape))
    flops = 2 * steps * double * slots * lanes * (depth + rows)
    return pl.pallas_call(
        functools.partial(forward_kernel, height),
        grid=(steps,),
        out_shape=jax.ShapeDtypeStruct((steps * chunk, rows, 2 * channels), jnp.bfloat16),
        in_specs=[
            whole(arrived.shape),
            pl.BlockSpec((1, double, depth), lambda step: (step, 0, 0)),
            whole(y_wave.shape),
        ],
        out_specs=pl.BlockSpec((chunk, rows, 2 * channels), lambda step: (step, 0, 0)),
        scratch_shapes=[pltpu.VMEM((lanes // LANES, double * (slots + 8), LANES), jnp.float32)],
        compiler_params=pltpu.CompilerParams(vmem_limit_bytes=VMEM_LIMIT),
        cost_estimate=pl.CostEstimate(
            flops=flops, bytes_accessed=16 * 1024 * 1024, transcendentals=0
        ),
    )(arrived, x_wave, y_wave)


def mix_kernel(*refs):
    spectra, (weight, out, held) = refs[:-3], refs[-3:]
    _, rows, lanes = spectra[0].shape
    count = pl.num_programs(0)
    step = pl.program_id(0)
    stride = held.shape[0] // rows
    channels = lanes // 2
    row = lax.broadcasted_iota(jnp.int32, (ZL, lanes), 0)
    lane = lax.broadcasted_iota(jnp.int32, (ZL, lanes), 1)
    keep = (row < HALF_Z) == (lane < channels)
    for mode in range(MODES):
        at = slice(mode * ZL, (mode + 1) * ZL)
        total = spectra[0][0, at].astype(jnp.float32)
        for source in spectra[1:]:
            total = total + source[0, at].astype(jnp.float32)
        high = total.astype(jnp.bfloat16).astype(jnp.float32)
        split = jnp.concatenate([high, total - high], axis=0).astype(jnp.bfloat16)
        plain = weight[0, mode]
        turned = jnp.concatenate([-plain[:, channels:], plain[:, :channels]], axis=1)
        mixed = dot(split, jnp.concatenate([plain, turned], axis=0))
        mixed = mixed[:ZL] + mixed[ZL:]
        other = pltpu.roll(pltpu.roll(mixed, HALF_Z, 0), channels, 1)
        held[pl.ds(mode * ZL * stride + step, ZL, stride=stride), :] = jnp.where(
            keep, mixed, other
        )

    @pl.when(step == count - 1)
    def _():
        out[...] = held[...].reshape(out.shape).astype(jnp.bfloat16)


def mix(spectra, weight):
    own, rows, lanes = spectra[0].shape
    return pl.pallas_call(
        mix_kernel,
        grid=(own,),
        out_shape=jax.ShapeDtypeStruct((rows, own, lanes), jnp.bfloat16),
        in_specs=[
            *[pl.BlockSpec((1, rows, lanes), lambda step: (step, 0, 0)) for _ in spectra],
            pl.BlockSpec((1,) + weight.shape[1:], lambda step: (step, 0, 0, 0)),
        ],
        out_specs=pl.BlockSpec((rows, own, lanes), lambda step: (0, 0, 0)),
        scratch_shapes=[pltpu.VMEM((rows * own, lanes), jnp.float32)],
        compiler_params=pltpu.CompilerParams(vmem_limit_bytes=VMEM_LIMIT),
    )(*spectra, weight)


def backward_kernel(height, mixed, terms, x_back, y_back, layer_mask, skip, out, held):
    sources, rows, own, lanes = mixed.shape
    width = x_back.shape[0] // 2
    channels = lanes // 2
    per_step = out.shape[0]
    step = pl.program_id(0)

    @pl.when(step == 0)
    def _():
        def mode(index, carry):
            for layer in range(HALF_Z):
                modes = jnp.concatenate(
                    [
                        mixed[source, index * ZL + part * HALF_Z + layer]
                        for part in range(2)
                        for source in range(sources)
                    ],
                    axis=0,
                )
                held[layer, pl.ds(index, 2 * width, stride=MODES), :] = dot(
                    x_back[...], jnp.concatenate([modes, modes], axis=0)
                )
            return carry

        lax.fori_loop(0, MODES, mode, 0, unroll=2)

    for inner in range(per_step):
        x = step * per_step + inner
        wave = [
            jnp.concatenate(
                [
                    held[
                        layer,
                        pl.ds(pl.multiple_of((part * width + x) * MODES, MODES), MODES),
                        :,
                    ]
                    for layer in range(HALF_Z)
                ],
                axis=1,
            )
            for part in range(2)
        ]
        wave = jnp.concatenate(wave, axis=0)
        high = wave.astype(jnp.bfloat16)
        parts = [high, (wave - high.astype(jnp.float32)).astype(jnp.bfloat16), high]
        skipped = dot(terms[inner], skip[...]).astype(jnp.bfloat16)
        for row in range(height):
            piece = skipped[:, row * channels : (row + 1) * channels]
            pair = jnp.concatenate([piece, piece], axis=1)
            parts.append(jnp.concatenate([pair] * HALF_Z, axis=1) * layer_mask[...])
        value = dot(y_back[...], jnp.concatenate(parts, axis=0))
        out[inner] = (0.5 * value * (1.0 + lax.erf(value * math.sqrt(0.5)))).astype(jnp.bfloat16)


def backward(mixed, terms, x_back, y_back, layer_mask, skip, height, per_step):
    width, slots, lanes = terms.shape
    whole = lambda shape: pl.BlockSpec(shape, lambda step: (0,) * len(shape))
    depth = layer_mask.shape[1]
    return pl.pallas_call(
        functools.partial(backward_kernel, height),
        grid=(width // per_step,),
        out_shape=jax.ShapeDtypeStruct((width, NY, depth), jnp.bfloat16),
        in_specs=[
            whole(mixed.shape),
            pl.BlockSpec((per_step, slots, lanes), lambda step: (step, 0, 0)),
            whole(x_back.shape),
            whole(y_back.shape),
            whole(layer_mask.shape),
            whole(skip.shape),
        ],
        out_specs=pl.BlockSpec((per_step, NY, depth), lambda step: (step, 0, 0)),
        scratch_shapes=[pltpu.VMEM((HALF_Z, 2 * width * MODES, mixed.shape[3]), jnp.float32)],
        compiler_params=pltpu.CompilerParams(vmem_limit_bytes=VMEM_LIMIT),
    )(mixed, terms, x_back, y_back, layer_mask, skip)


def split(value, axis):
    high = value.astype(jnp.bfloat16)
    low = (value - high.astype(jnp.float32)).astype(jnp.bfloat16)
    return jnp.concatenate([high, low], axis=axis)


def angle(phase, length):
    return (phase % length).astype(jnp.float32) * (2.0 * math.pi / length)


def per_device(
    point_features,
    point_position,
    block_counts,
    pair_tile,
    pair_offset,
    skip_weight,
    spectral_weight,
):
    pencils = lax.axis_size("pencil")
    owners = lax.axis_size("point")
    pencil = lax.axis_index("pencil")
    me = lax.axis_index("point")
    channels = skip_weight.shape[0]
    width = NX // pencils
    height = TILE_CELLS // width
    row_blocks = NY // height
    tiles_dev = ZL * row_blocks
    slots = owners * CAP
    own = KMODES // pencils
    lanes = height * channels
    bf16 = jnp.bfloat16

    row_tiles = lax.all_gather(pair_tile, "point")
    terms = make_terms(
        point_features,
        point_position,
        block_counts,
        pair_tile,
        pair_offset,
        owners,
        width,
        height,
        tiles_dev,
    )
    arrived = lax.all_to_all(terms, "point", split_axis=0, concat_axis=0, tiled=True)

    mine = (row_tiles // tiles_dev == me).astype(jnp.int32)
    place = jnp.cumsum(mine, axis=1) - 1
    hit = (place[:, :, None] == jnp.arange(CAP, dtype=jnp.int32)) & (mine[:, :, None] == 1)
    labels = (
        jnp.sum(jnp.where(hit, (row_tiles % tiles_dev + 1)[:, :, None], 0), axis=1) - 1
    ).reshape(slots)
    layer_of = jnp.where(labels >= 0, labels // row_blocks, -1)
    block_of = labels % row_blocks

    modes = jnp.arange(MODES, dtype=jnp.int32)
    x_index = jnp.arange(KMODES, dtype=jnp.int32)
    x_freqs = jnp.where(x_index < MODES, x_index, NX - KMODES + x_index)
    x_cells = pencil * width + jnp.arange(width, dtype=jnp.int32)
    x_angle = angle(x_freqs[:, None] * x_cells[None, :], NX)
    x_cos, x_sin = jnp.cos(x_angle), jnp.sin(x_angle)
    cores = 2
    chips = pencils // cores
    chip, core = pencil // cores, pencil % cores
    chunk = own if slots * lanes * own * 8 <= 8 * 1024 * 1024 else 4

    def x_wave(dests):
        index = jnp.concatenate([dest * own + jnp.arange(own, dtype=jnp.int32) for dest in dests])
        phase = angle(x_freqs[index][:, None] * x_cells[None, :], NX)
        steps = index.shape[0] // chunk
        table = split(jnp.stack([jnp.cos(phase), -jnp.sin(phase)]), 2)
        table = table.reshape(2, steps, chunk, 2 * width).transpose(1, 0, 2, 3)
        return table.reshape(steps, 2 * chunk, 2 * width)

    x_back = jnp.concatenate(
        [
            jnp.concatenate([x_cos.T, -x_sin.T], axis=1),
            jnp.concatenate([x_sin.T, x_cos.T], axis=1),
        ],
        axis=0,
    )
    x_back = split(x_back, 1)

    pair_y = block_of[None, :] * height + jnp.arange(height, dtype=jnp.int32)[:, None]
    y_angle = angle(modes[None, :, None] * pair_y[:, None, :], NY)
    y_cos, y_sin = jnp.cos(y_angle).astype(bf16), jnp.sin(y_angle).astype(bf16)
    order = jnp.arange(ZL, dtype=jnp.int32)
    order = order % HALF_Z * 2 + order // HALF_Z
    layer_hit = layer_of[None, :] == order[:, None]
    turned = jnp.stack(
        [
            jnp.stack([y_cos, y_sin], axis=2),
            jnp.stack([-y_sin, y_cos], axis=2),
        ],
        axis=1,
    )
    y_wave = jnp.where(
        layer_hit[None, None, None, :, None, :], turned[:, :, :, None], jnp.zeros((), bf16)
    )
    y_wave = y_wave.transpose(1, 2, 3, 0, 4, 5).reshape(2 * MODES * ZL, height * 2 * slots)

    rows_y = jnp.arange(NY, dtype=jnp.int32)
    back_angle = angle(rows_y[:, None] * modes[None, :], NY)
    scale = jnp.where(modes == 0, 1.0, 2.0).astype(jnp.float32)[None, :] / (NX * NY)
    wave_back = jnp.concatenate([jnp.cos(back_angle), -jnp.sin(back_angle)], axis=1)
    wave_back = wave_back * jnp.concatenate([scale, scale], axis=1)
    wave_high = wave_back.astype(bf16)
    y_back = jnp.concatenate(
        [
            wave_high,
            wave_high,
            (wave_back - wave_high.astype(jnp.float32)).astype(bf16),
            (rows_y[:, None] == pair_y.reshape(-1)[None, :]).astype(bf16),
        ],
        axis=1,
    )
    lane_layer = jnp.arange(ZL * channels, dtype=jnp.int32) // channels
    layer_mask = (layer_of[:, None] == lane_layer[None, :]).astype(bf16)
    skip = jnp.kron(jnp.eye(height, dtype=bf16), skip_weight)

    def to_core(value):
        return lax.ppermute(
            value, "pencil", [(rank, rank // cores * cores + 1 - rank % cores) for rank in range(pencils)]
        )

    def dest(shift, other):
        return (chip + shift) % chips * cores + (1 - core if other else core)

    shifts = list(range(1, chips))
    for_other = forward(arrived, x_wave([dest(shift, True) for shift in shifts]), y_wave, height)
    from_other = to_core(for_other)
    for_own = forward(arrived, x_wave([dest(shift, False) for shift in shifts]), y_wave, height)
    sums = (for_own.astype(jnp.float32) + from_other.astype(jnp.float32)).astype(bf16)
    near = forward(arrived, x_wave([dest(0, True), dest(0, False)]), y_wave, height)
    spectra = [near[own:], to_core(near[:own])]
    for place, shift in enumerate(shifts):
        moves = [
            (rank, (rank // cores + shift) % chips * cores + rank % cores) for rank in range(pencils)
        ]
        spectra.append(lax.ppermute(sums[place * own : (place + 1) * own], "pencil", moves))
    mixed = mix(spectra, spectral_weight)
    gathered = lax.all_gather(mixed, "pencil")
    by_row = arrived.transpose(1, 0, 2)
    return backward(
        gathered, by_row, x_back, y_back, layer_mask, skip, height, 4 if width % 4 == 0 else 1
    )


def solution(mesh):
    placed = (
        P(None, ("groups", "pencil", "point")),
        P(None, ("groups", "pencil", "point")),
        P(("groups", "pencil", "point"), None),
        P(("groups", "pencil", "point")),
        P(None, ("groups", "pencil", "point")),
        P(),
        P("pencil", None, None, None),
    )
    return jax.shard_map(
        per_device,
        mesh=mesh,
        in_specs=placed,
        out_specs=P(("groups", "pencil"), None, "point"),
        check_vma=False,
    )
```

```python
import functools
import math

import jax
import jax.numpy as jnp
from jax import lax
from jax.experimental import pallas as pl
from jax.experimental.pallas import tpu as pltpu
from jax.sharding import PartitionSpec as P

NX = 256
NY = 256
MODES = 32
BLOCK = 128
TILE_CELLS = 128
ZL = 8
KMODES = 64
CAP = 32
HALF_Z = ZL // 2
LANES = 128
VMEM_LIMIT = 56 * 1024 * 1024


def dot(left, right):
    return jnp.dot(left, right, preferred_element_type=jnp.float32)


def terms_kernel(tiles_dev, counts, tiles, offsets, features, position, out, used):
    slots, width, lanes = out.shape
    channels = features.shape[0]
    height = lanes // channels
    owners = slots // CAP
    pairs = tiles.shape[0]
    for owner in range(owners):
        used[owner] = 0
    out[...] = jnp.zeros_like(out)
    cell_x = lax.broadcasted_iota(jnp.int32, (width, BLOCK), 0).astype(jnp.float32) + 0.5

    def one(pair, carry):
        block, end = carry
        moved = (pair >= end).astype(jnp.int32)
        block = block + moved
        end = end + moved * counts[0, block]
        at = pl.ds(pl.multiple_of(block * BLOCK, BLOCK), BLOCK)
        spot = position[:, at]
        gap_x = spot[0:1] * float(width) + offsets[0, pair] - cell_x
        along_x = jnp.exp(-(gap_x * gap_x))
        point_y = spot[1:2] * float(height) + offsets[1, pair]
        point_z = spot[2:3] - 0.5 + offsets[2, pair]
        square_z = point_z * point_z
        rows = []
        for row in range(height):
            gap_y = point_y - (row + 0.5)
            rows.append((along_x * jnp.exp(-(gap_y * gap_y + square_z))).astype(jnp.bfloat16))
        cells = jnp.concatenate(rows, axis=0)
        term = lax.dot_general(
            cells, features[:, at], (((1,), (1,)), ((), ())), preferred_element_type=jnp.float32
        )
        term = jnp.concatenate(
            [term[row * width : (row + 1) * width] for row in range(height)], axis=1
        )
        owner = tiles[pair] // tiles_dev
        slot = used[owner]
        used[owner] = slot + 1
        out[owner * CAP + slot] = term.astype(jnp.bfloat16)
        return block, end

    lax.fori_loop(0, pairs, one, (jnp.int32(0), counts[0, 0]), unroll=4)


def make_terms(features, position, counts, tiles, offsets, owners, width, height, tiles_dev):
    channels = features.shape[0]
    smem = pl.BlockSpec(memory_space=pltpu.SMEM)
    vmem = pl.BlockSpec(memory_space=pltpu.VMEM)
    return pl.pallas_call(
        functools.partial(terms_kernel, tiles_dev),
        out_shape=jax.ShapeDtypeStruct((owners * CAP, width, height * channels), jnp.bfloat16),
        in_specs=[smem, smem, smem, vmem, vmem],
        out_specs=vmem,
        scratch_shapes=[pltpu.SMEM((owners,), jnp.int32)],
        compiler_params=pltpu.CompilerParams(vmem_limit_bytes=VMEM_LIMIT),
    )(counts, tiles, offsets, features, position)


def forward_kernel(height, arrived, x_wave, y_wave, out, held):
    slots, width, lanes = arrived.shape
    parts = x_wave.shape[1]
    steps = parts // 2
    rows = out.shape[1]
    groups = lanes // LANES
    channels = lanes // height
    per_group = LANES // channels
    stride = held.shape[1] // parts
    first_half = lax.broadcasted_iota(jnp.int32, (1, LANES), 1) < channels

    def one(slot, carry):
        cells = arrived[slot]
        wave = dot(x_wave[0], jnp.concatenate([cells, cells], axis=0))
        for group in range(groups):
            held[group, pl.ds(slot, parts, stride=stride), :] = wave[
                :, group * LANES : (group + 1) * LANES
            ]
        return carry

    lax.fori_loop(0, slots, one, 0, unroll=8)

    def both(index, group):
        return jnp.concatenate(
            [
                held[
                    group,
                    pl.ds(pl.multiple_of((index + part * steps) * stride, 8), slots),
                    :,
                ]
                for part in range(2)
            ],
            axis=0,
        )

    def modes(index, carry):
        base = index * 4
        columns = []
        for pair in range(2):
            pieces = []
            for group in range(groups):
                left, right = both(base + 2 * pair, group), both(base + 2 * pair + 1, group)
                left_turned = pltpu.roll(left, channels, 1)
                right_turned = pltpu.roll(right, channels, 1)
                pieces.append(jnp.where(first_half, left, right_turned).astype(jnp.bfloat16))
                pieces.append(jnp.where(first_half, left_turned, right).astype(jnp.bfloat16))
            columns.append(jnp.concatenate(pieces, axis=0))
        total = dot(y_wave[...], jnp.concatenate(columns, axis=1))
        for pair in range(2):
            real = total[:rows, pair * LANES : (pair + 1) * LANES]
            imag = total[rows:, pair * LANES : (pair + 1) * LANES]
            out[base + 2 * pair] = jnp.where(
                first_half, real, pltpu.roll(imag, channels, 1)
            ).astype(jnp.bfloat16)
            out[base + 2 * pair + 1] = jnp.where(
                first_half, pltpu.roll(real, channels, 1), imag
            ).astype(jnp.bfloat16)
        return carry

    lax.fori_loop(0, steps // 4, modes, 0)


def forward(arrived, x_wave, y_wave, height):
    slots, width, lanes = arrived.shape
    channels = lanes // height
    rows = y_wave.shape[0] // 2
    steps, double, depth = x_wave.shape
    chunk = double // 2
    whole = lambda shape: pl.BlockSpec(shape, lambda step: (0,) * len(shape))
    flops = 2 * steps * double * slots * lanes * (depth + rows)
    return pl.pallas_call(
        functools.partial(forward_kernel, height),
        grid=(steps,),
        out_shape=jax.ShapeDtypeStruct((steps * chunk, rows, 2 * channels), jnp.bfloat16),
        in_specs=[
            whole(arrived.shape),
            pl.BlockSpec((1, double, depth), lambda step: (step, 0, 0)),
            whole(y_wave.shape),
        ],
        out_specs=pl.BlockSpec((chunk, rows, 2 * channels), lambda step: (step, 0, 0)),
        scratch_shapes=[pltpu.VMEM((lanes // LANES, double * (slots + 8), LANES), jnp.float32)],
        compiler_params=pltpu.CompilerParams(vmem_limit_bytes=VMEM_LIMIT),
        cost_estimate=pl.CostEstimate(
            flops=flops, bytes_accessed=16 * 1024 * 1024, transcendentals=0
        ),
    )(arrived, x_wave, y_wave)


def mix_kernel(*refs):
    spectra, (weight, out, held) = refs[:-3], refs[-3:]
    _, rows, lanes = spectra[0].shape
    count = pl.num_programs(0)
    step = pl.program_id(0)
    stride = held.shape[0] // rows
    channels = lanes // 2
    row = lax.broadcasted_iota(jnp.int32, (ZL, lanes), 0)
    lane = lax.broadcasted_iota(jnp.int32, (ZL, lanes), 1)
    keep = (row < HALF_Z) == (lane < channels)
    for mode in range(MODES):
        at = slice(mode * ZL, (mode + 1) * ZL)
        total = spectra[0][0, at].astype(jnp.float32)
        for source in spectra[1:]:
            total = total + source[0, at].astype(jnp.float32)
        high = total.astype(jnp.bfloat16).astype(jnp.float32)
        split = jnp.concatenate([high, total - high], axis=0).astype(jnp.bfloat16)
        plain = weight[0, mode]
        turned = jnp.concatenate([-plain[:, channels:], plain[:, :channels]], axis=1)
        mixed = dot(split, jnp.concatenate([plain, turned], axis=0))
        mixed = mixed[:ZL] + mixed[ZL:]
        other = pltpu.roll(pltpu.roll(mixed, HALF_Z, 0), channels, 1)
        held[pl.ds(mode * ZL * stride + step, ZL, stride=stride), :] = jnp.where(
            keep, mixed, other
        )

    @pl.when(step == count - 1)
    def _():
        out[...] = held[...].reshape(out.shape).astype(jnp.bfloat16)


def mix(spectra, weight):
    own, rows, lanes = spectra[0].shape
    return pl.pallas_call(
        mix_kernel,
        grid=(own,),
        out_shape=jax.ShapeDtypeStruct((rows, own, lanes), jnp.bfloat16),
        in_specs=[
            *[pl.BlockSpec((1, rows, lanes), lambda step: (step, 0, 0)) for _ in spectra],
            pl.BlockSpec((1,) + weight.shape[1:], lambda step: (step, 0, 0, 0)),
        ],
        out_specs=pl.BlockSpec((rows, own, lanes), lambda step: (0, 0, 0)),
        scratch_shapes=[pltpu.VMEM((rows * own, lanes), jnp.float32)],
        compiler_params=pltpu.CompilerParams(vmem_limit_bytes=VMEM_LIMIT),
    )(*spectra, weight)


def backward_kernel(height, mixed, terms, x_back, y_back, layer_mask, skip, out, held):
    sources, rows, own, lanes = mixed.shape
    width = x_back.shape[0] // 2
    channels = lanes // 2
    per_step = out.shape[0]
    step = pl.program_id(0)

    @pl.when(step == 0)
    def _():
        def mode(index, carry):
            for layer in range(HALF_Z):
                modes = jnp.concatenate(
                    [
                        mixed[source, index * ZL + part * HALF_Z + layer]
                        for part in range(2)
                        for source in range(sources)
                    ],
                    axis=0,
                )
                held[layer, pl.ds(index, 2 * width, stride=MODES), :] = dot(
                    x_back[...], jnp.concatenate([modes, modes], axis=0)
                )
            return carry

        lax.fori_loop(0, MODES, mode, 0, unroll=2)

    for inner in range(per_step):
        x = step * per_step + inner
        wave = [
            jnp.concatenate(
                [
                    held[
                        layer,
                        pl.ds(pl.multiple_of((part * width + x) * MODES, MODES), MODES),
                        :,
                    ]
                    for layer in range(HALF_Z)
                ],
                axis=1,
            )
            for part in range(2)
        ]
        wave = jnp.concatenate(wave, axis=0)
        high = wave.astype(jnp.bfloat16)
        parts = [high, (wave - high.astype(jnp.float32)).astype(jnp.bfloat16), high]
        skipped = dot(terms[inner], skip[...]).astype(jnp.bfloat16)
        for row in range(height):
            piece = skipped[:, row * channels : (row + 1) * channels]
            pair = jnp.concatenate([piece, piece], axis=1)
            parts.append(jnp.concatenate([pair] * HALF_Z, axis=1) * layer_mask[...])
        value = dot(y_back[...], jnp.concatenate(parts, axis=0))
        out[inner] = (0.5 * value * (1.0 + lax.erf(value * math.sqrt(0.5)))).astype(jnp.bfloat16)


def backward(mixed, terms, x_back, y_back, layer_mask, skip, height, per_step):
    width, slots, lanes = terms.shape
    whole = lambda shape: pl.BlockSpec(shape, lambda step: (0,) * len(shape))
    depth = layer_mask.shape[1]
    return pl.pallas_call(
        functools.partial(backward_kernel, height),
        grid=(width // per_step,),
        out_shape=jax.ShapeDtypeStruct((width, NY, depth), jnp.bfloat16),
        in_specs=[
            whole(mixed.shape),
            pl.BlockSpec((per_step, slots, lanes), lambda step: (step, 0, 0)),
            whole(x_back.shape),
            whole(y_back.shape),
            whole(layer_mask.shape),
            whole(skip.shape),
        ],
        out_specs=pl.BlockSpec((per_step, NY, depth), lambda step: (step, 0, 0)),
        scratch_shapes=[pltpu.VMEM((HALF_Z, 2 * width * MODES, mixed.shape[3]), jnp.float32)],
        compiler_params=pltpu.CompilerParams(vmem_limit_bytes=VMEM_LIMIT),
    )(mixed, terms, x_back, y_back, layer_mask, skip)


def split(value, axis):
    high = value.astype(jnp.bfloat16)
    low = (value - high.astype(jnp.float32)).astype(jnp.bfloat16)
    return jnp.concatenate([high, low], axis=axis)


def angle(phase, length):
    return (phase % length).astype(jnp.float32) * (2.0 * math.pi / length)


def per_device(
    point_features,
    point_position,
    block_counts,
    pair_tile,
    pair_offset,
    skip_weight,
    spectral_weight,
):
    pencils = lax.axis_size("pencil")
    owners = lax.axis_size("point")
    pencil = lax.axis_index("pencil")
    me = lax.axis_index("point")
    channels = skip_weight.shape[0]
    width = NX // pencils
    height = TILE_CELLS // width
    row_blocks = NY // height
    tiles_dev = ZL * row_blocks
    slots = owners * CAP
    own = KMODES // pencils
    lanes = height * channels
    bf16 = jnp.bfloat16

    row_tiles = lax.all_gather(pair_tile, "point")
    terms = make_terms(
        point_features,
        point_position,
        block_counts,
        pair_tile,
        pair_offset,
        owners,
        width,
        height,
        tiles_dev,
    )
    arrived = lax.all_to_all(terms, "point", split_axis=0, concat_axis=0, tiled=True)

    mine = (row_tiles // tiles_dev == me).astype(jnp.int32)
    place = jnp.cumsum(mine, axis=1) - 1
    hit = (place[:, :, None] == jnp.arange(CAP, dtype=jnp.int32)) & (mine[:, :, None] == 1)
    labels = (
        jnp.sum(jnp.where(hit, (row_tiles % tiles_dev + 1)[:, :, None], 0), axis=1) - 1
    ).reshape(slots)
    layer_of = jnp.where(labels >= 0, labels // row_blocks, -1)
    block_of = labels % row_blocks

    modes = jnp.arange(MODES, dtype=jnp.int32)
    x_index = jnp.arange(KMODES, dtype=jnp.int32)
    x_freqs = jnp.where(x_index < MODES, x_index, NX - KMODES + x_index)
    x_cells = pencil * width + jnp.arange(width, dtype=jnp.int32)
    x_angle = angle(x_freqs[:, None] * x_cells[None, :], NX)
    x_cos, x_sin = jnp.cos(x_angle), jnp.sin(x_angle)
    cores = 2
    chips = pencils // cores
    chip, core = pencil // cores, pencil % cores
    chunk = own if slots * lanes * own * 8 <= 8 * 1024 * 1024 else 4

    def x_wave(dests):
        index = jnp.concatenate([dest * own + jnp.arange(own, dtype=jnp.int32) for dest in dests])
        phase = angle(x_freqs[index][:, None] * x_cells[None, :], NX)
        steps = index.shape[0] // chunk
        table = split(jnp.stack([jnp.cos(phase), -jnp.sin(phase)]), 2)
        table = table.reshape(2, steps, chunk, 2 * width).transpose(1, 0, 2, 3)
        return table.reshape(steps, 2 * chunk, 2 * width)

    x_back = jnp.concatenate(
        [
            jnp.concatenate([x_cos.T, -x_sin.T], axis=1),
            jnp.concatenate([x_sin.T, x_cos.T], axis=1),
        ],
        axis=0,
    )
    x_back = split(x_back, 1)

    pair_y = block_of[None, :] * height + jnp.arange(height, dtype=jnp.int32)[:, None]
    y_angle = angle(modes[None, :, None] * pair_y[:, None, :], NY)
    y_cos, y_sin = jnp.cos(y_angle).astype(bf16), jnp.sin(y_angle).astype(bf16)
    order = jnp.arange(ZL, dtype=jnp.int32)
    order = order % HALF_Z * 2 + order // HALF_Z
    layer_hit = layer_of[None, :] == order[:, None]
    turned = jnp.stack(
        [
            jnp.stack([y_cos, y_sin], axis=2),
            jnp.stack([-y_sin, y_cos], axis=2),
        ],
        axis=1,
    )
    y_wave = jnp.where(
        layer_hit[None, None, None, :, None, :], turned[:, :, :, None], jnp.zeros((), bf16)
    )
    y_wave = y_wave.transpose(1, 2, 3, 0, 4, 5).reshape(2 * MODES * ZL, height * 2 * slots)

    rows_y = jnp.arange(NY, dtype=jnp.int32)
    back_angle = angle(rows_y[:, None] * modes[None, :], NY)
    scale = jnp.where(modes == 0, 1.0, 2.0).astype(jnp.float32)[None, :] / (NX * NY)
    wave_back = jnp.concatenate([jnp.cos(back_angle), -jnp.sin(back_angle)], axis=1)
    wave_back = wave_back * jnp.concatenate([scale, scale], axis=1)
    wave_high = wave_back.astype(bf16)
    y_back = jnp.concatenate(
        [
            wave_high,
            wave_high,
            (wave_back - wave_high.astype(jnp.float32)).astype(bf16),
            (rows_y[:, None] == pair_y.reshape(-1)[None, :]).astype(bf16),
        ],
        axis=1,
    )
    lane_layer = jnp.arange(ZL * channels, dtype=jnp.int32) // channels
    layer_mask = (layer_of[:, None] == lane_layer[None, :]).astype(bf16)
    skip = jnp.kron(jnp.eye(height, dtype=bf16), skip_weight)

    def to_core(value):
        return lax.ppermute(
            value, "pencil", [(rank, rank // cores * cores + 1 - rank % cores) for rank in range(pencils)]
        )

    def dest(shift, other):
        return (chip + shift) % chips * cores + (1 - core if other else core)

    shifts = list(range(1, chips))
    for_other = forward(arrived, x_wave([dest(shift, True) for shift in shifts]), y_wave, height)
    from_other = to_core(for_other)
    for_own = forward(arrived, x_wave([dest(shift, False) for shift in shifts]), y_wave, height)
    sums = (for_own.astype(jnp.float32) + from_other.astype(jnp.float32)).astype(bf16)
    later, sums = lax.optimization_barrier((arrived, sums))
    near = forward(later, x_wave([dest(0, True), dest(0, False)]), y_wave, height)
    spectra = [near[own:], to_core(near[:own])]
    for place, shift in enumerate(shifts):
        moves = [
            (rank, (rank // cores + shift) % chips * cores + rank % cores) for rank in range(pencils)
        ]
        spectra.append(lax.ppermute(sums[place * own : (place + 1) * own], "pencil", moves))
    mixed = mix(spectra, spectral_weight)
    gathered = lax.all_gather(mixed, "pencil")
    by_row = arrived.transpose(1, 0, 2)
    return backward(
        gathered, by_row, x_back, y_back, layer_mask, skip, height, 4 if width % 4 == 0 else 1
    )


def solution(mesh):
    placed = (
        P(None, ("groups", "pencil", "point")),
        P(None, ("groups", "pencil", "point")),
        P(("groups", "pencil", "point"), None),
        P(("groups", "pencil", "point")),
        P(None, ("groups", "pencil", "point")),
        P(),
        P("pencil", None, None, None),
    )
    return jax.shard_map(
        per_device,
        mesh=mesh,
        in_specs=placed,
        out_specs=P(("groups", "pencil"), None, "point"),
        check_vma=False,
    )
```
